128 devices in a mesh: col: 16 (over x, z), row: 8 (over y, core).
Axes of the slice: x: 4, y: 4, z: 4, core: 2. Of those that a mesh axis runs over, the one named last changes fastest.
Arguments:
- tokens: bfloat16 [16384, 2048], P(('col', 'row')), may hold values from -6 to 6
- route_weight: float32 [16384, 4], P(('col', 'row')), may hold values from 0.1 to 1
- expert_ids: int32 [16384, 4], P(('col', 'row')), may hold values from 0 to 127, all different within a row; in each aligned block of 128 rows (0 to 127, 128 to 255, ...) at most 8 rows name the same one
- placement: int32 [128], replicated, may hold values from 0 to 127, each once
- w_gate: bfloat16 [128, 2048, 768], P(('col', 'row')), may hold values from -0.125 to 0.125
- w_up: bfloat16 [128, 2048, 768], P(('col', 'row')), may hold values from -0.125 to 0.125
- w_down: bfloat16 [128, 768, 2048], P(('col', 'row')), may hold values from -0.21875 to 0.21875
- cotangent: bfloat16 [16384, 2048], P(('col', 'row')), may hold values from -0.59765625 to 0.59765625
Outputs:
- mixed: bfloat16 [16384, 2048], P(('col', 'row'))
- grad_tokens: bfloat16 [16384, 2048], P(('col', 'row'))
- grad_route: float32 [16384, 4], P(('col', 'row'))
- grad_gate: bfloat16 [128, 2048, 768], P(('col', 'row'))
- grad_up: bfloat16 [128, 2048, 768], P(('col', 'row'))
- grad_down: bfloat16 [128, 768, 2048], P(('col', 'row'))
The draws below stay inside these ranges and needn't reach their ends.
Inputs may be any that keep to these rules, and one draw needn't show every extreme that they name: `expert_ids`: in each aligned block of 128 rows (the tokens of one device) every expert is named at most 8 times, a bound that some block reaches. `placement`: each expert slot serves exactly one expert.
All inputs are finite; a program needn't handle non-finite values.
Results may differ from the reference program's by a relative error of at most 0.0064.
Values may be sent and summed in bfloat16 or wider, within the bound.
No kernel may reach another device: no remote copies, remote signals or barrier semaphores. Data moves between devices by JAX's collectives and lax.ppermute only.
A program may use at most 128 MiB of HBM per device.

```python
import math
import jax
import jax.numpy as jnp
import numpy as np
from jax import lax

D = 2048
FF = 768
TOP = 4
TOK_DEV = 128
EXPERTS = 128
TOKENS = 16384
CAP = 8
N_COL = 16
N_ROW = 8


def steps_of(rng, dims, cuts, least, top_value):
    factor_of = 1.0
    for dim, shards_of in cuts:
        heights = jax.random.uniform(jax.random.fold_in(jax.random.fold_in(rng, 6), dim), (shards_of,), jnp.float32, least / len(cuts), top_value / len(cuts))
        factor_of = factor_of * jnp.repeat(jnp.exp(heights), dims[dim] // shards_of).reshape((-1,) + (1,) * (len(dims) - 1 - dim))
    return factor_of


def shared_out(key, own, number, rows, amount, top, most, slope):
    order = jax.random.permutation(key, amount)
    heavy_load, usual = portions_of(amount, rows * top, most, slope, True), portions_of(amount, rows * top, most, slope, False)
    places = jnp.arange(amount)

    def named(sizes, offset_by):
        used = int((sizes > 0).sum())
        fixed = max(1, used // 4)
        shifted = fixed + (places - fixed + offset_by * (used - fixed)) % max(1, amount - fixed)
        return jnp.zeros((amount,), jnp.int32).at[order[jnp.where(places < fixed, places, shifted)]].set(jnp.asarray(sizes, jnp.int32))

    sizes = jnp.where(number % 4 == 0, named(heavy_load, number // 4), named(usual, number - number // 4 - 1))
    mixed = jax.random.permutation(jax.random.fold_in(own, 3), amount)
    giver, sink = mixed[0:amount // 2 * 2:2], mixed[1:amount // 2 * 2:2]
    margin = jnp.minimum(sizes[giver] - 1, most - sizes[sink]) // 2
    margin = jnp.where((giver == order[0]) | (sink == order[0]) | (sizes[sink] == 0), 0, jnp.maximum(margin, 0))
    shifted = jax.random.randint(jax.random.fold_in(own, 4), (amount // 2,), 0, 1 << 20) % (margin + 1)
    sizes = sizes.at[giver].add(-shifted).at[sink].add(shifted)
    labels = jnp.searchsorted(jnp.cumsum(sizes), jnp.arange(rows * top), side="right").astype(jnp.int32)
    listing = labels.reshape(top, rows).T
    listing = listing[jax.random.permutation(jax.random.fold_in(own, 1), rows)]
    offset_by = jax.random.randint(jax.random.fold_in(own, 2), (rows, 1), 0, top)
    return jnp.take_along_axis(listing, (jnp.arange(top)[None, :] + offset_by) % top, axis=1)


def portions_of(number_of, total, reach, slope, full):
    loads = [(1 << 20) // math.isqrt(standing ** slope) + 1 for standing in range(1, number_of + 1)]
    largest = reach if full else min(reach, max(-(-total // number_of), total * loads[0] // sum(loads)))
    least = 1 if total - largest >= number_of - 1 else 0
    given, rest = [largest] + [least] * (number_of - 1), total - largest - least * (number_of - 1)
    while rest > 0:
        candidates = [i for i in range(1, number_of) if given[i] < largest] or [i for i in range(1, number_of) if given[i] < reach]
        mass, remaining = sum([loads[i] for i in candidates]), rest
        for i in candidates:
            more = min(reach - given[i], max(1, remaining * loads[i] // mass), rest)
            given[i] = given[i] + more
            rest = rest - more
    return np.array(given)


def gaussian(own_key, dims, deviation, reach, cuts=(), kind=jnp.bfloat16):
    entries = deviation * jax.random.normal(own_key, dims, jnp.float32)
    if cuts:
        entries = entries * steps_of(own_key, dims, cuts, -0.22, 0.18)
    return jnp.clip(entries, -reach, reach).astype(kind)


def setup_inputs(seed: int = 0) -> dict:
    key_list = jax.random.split(jax.random.key(seed), 9)
    tokens = gaussian(key_list[0], (TOKENS, D), 1.0, 6.0, ((0, 128),))
    route_weight = jnp.clip(0.1 + 0.9 * jax.random.uniform(key_list[1], (TOKENS, TOP), jnp.float32) ** steps_of(key_list[1], (TOKENS, TOP), ((0, 128),), -0.2, 0.2), 0.1, 1.0)
    expert_ids_keys = jax.random.split(jax.random.fold_in(key_list[2], 1), TOKENS // TOK_DEV)
    expert_ids_turns = jax.random.permutation(jax.random.fold_in(key_list[2], 3), TOKENS // TOK_DEV)
    expert_ids = jax.vmap(lambda own, number: shared_out(jax.random.fold_in(key_list[2], 2), own, number, TOK_DEV, EXPERTS, TOP, CAP, 2))(expert_ids_keys, expert_ids_turns).reshape((TOKENS, TOP))
    placement = jax.random.permutation(key_list[3], EXPERTS).astype(jnp.int32)
    w_gate = gaussian(key_list[4], (EXPERTS, D, FF), D ** -0.5, 0.125, ((0, 128),))
    w_up = gaussian(key_list[5], (EXPERTS, D, FF), D ** -0.5, 0.125, ((0, 128),))
    w_down = gaussian(key_list[6], (EXPERTS, FF, D), FF ** -0.5, 0.21875, ((0, 128),))
    cotangent = gaussian(key_list[7], (TOKENS, D), 0.1, 0.59765625, ((0, 128),))
    return dict(tokens=tokens, route_weight=route_weight, expert_ids=expert_ids, placement=placement, w_gate=w_gate, w_up=w_up, w_down=w_down, cotangent=cotangent)


def expert_forward(inputs, weight_gate, weight_up, weight_down):
    gate_pre = jnp.dot(inputs, weight_gate, preferred_element_type=jnp.float32)
    up_proj = jnp.dot(inputs, weight_up, preferred_element_type=jnp.float32)
    hidden = (gate_pre * jax.nn.sigmoid(gate_pre) * up_proj).astype(jnp.bfloat16)
    outcome = jnp.dot(hidden, weight_down, preferred_element_type=jnp.float32).astype(jnp.bfloat16)
    return outcome, gate_pre, up_proj, hidden


def expert_backward(inputs, scaled_cot, gate_pre, up_proj, hidden, weight_gate, weight_up, weight_down):
    d_hidden = jnp.dot(scaled_cot, weight_down.T, preferred_element_type=jnp.float32)
    sigmoid_val = jax.nn.sigmoid(gate_pre)
    d_gate = (d_hidden * up_proj * sigmoid_val * (1.0 + gate_pre * (1.0 - sigmoid_val))).astype(jnp.bfloat16)
    d_up = (d_hidden * gate_pre * sigmoid_val).astype(jnp.bfloat16)
    d_inputs = (jnp.dot(d_gate, weight_gate.T, preferred_element_type=jnp.float32)
                + jnp.dot(d_up, weight_up.T, preferred_element_type=jnp.float32)).astype(jnp.bfloat16)
    contract = (((0,), (0,)), ((), ()))
    grad_gate = lax.dot_general(inputs, d_gate, contract, preferred_element_type=jnp.float32).astype(jnp.bfloat16)
    grad_up = lax.dot_general(inputs, d_up, contract, preferred_element_type=jnp.float32).astype(jnp.bfloat16)
    grad_down = lax.dot_general(hidden, scaled_cot, contract, preferred_element_type=jnp.float32).astype(jnp.bfloat16)
    return d_inputs, grad_gate, grad_up, grad_down


def reference(tokens, route_weight, expert_ids, placement, w_gate, w_up, w_down, cotangent):
    devices = N_COL * N_ROW
    per_dev = TOK_DEV * TOP
    expert_grid = jnp.arange(EXPERTS, dtype=jnp.int32)
    target = jnp.sum(jnp.where(expert_ids[..., None] == expert_grid, placement, 0), -1).astype(jnp.int32)
    targets = target.reshape(devices, per_dev)
    one_hot = (targets[..., None] == expert_grid).astype(jnp.int32)
    position = jnp.sum((jnp.cumsum(one_hot, 1) - one_hot) * one_hot, -1).astype(jnp.int32)
    source_dev = jnp.broadcast_to(jnp.arange(devices, dtype=jnp.int32)[:, None], (devices, per_dev))
    route_index = jnp.arange(TOKENS * TOP, dtype=jnp.int32).reshape(devices, per_dev)
    slot_route = jnp.full((EXPERTS, devices, CAP), TOKENS * TOP, jnp.int32)
    slot_route = slot_route.at[targets, source_dev, position].set(route_index)
    slot_token = (slot_route // TOP).astype(jnp.int32)
    padded_tokens = jnp.concatenate([tokens, jnp.zeros((1, D), jnp.bfloat16)], 0)
    scaled = (route_weight[..., None] * cotangent[:, None, :].astype(jnp.float32)).astype(jnp.bfloat16)
    padded_scaled = jnp.concatenate([scaled.reshape(TOKENS * TOP, D), jnp.zeros((1, D), jnp.bfloat16)], 0)

    def per_expert(items):
        weight_gate, weight_up, weight_down, token_rows, route_rows = items
        inputs = padded_tokens[token_rows.reshape(-1)]
        scaled_cot = padded_scaled[route_rows.reshape(-1)]
        outcome, gate_pre, up_proj, hidden = expert_forward(inputs, weight_gate, weight_up, weight_down)
        d_inputs, grad_gate, grad_up, grad_down = expert_backward(
            inputs, scaled_cot, gate_pre, up_proj, hidden, weight_gate, weight_up, weight_down)
        return outcome, d_inputs, grad_gate, grad_up, grad_down

    outcome, d_inputs, grad_gate, grad_up, grad_down = lax.map(
        per_expert, (w_gate, w_up, w_down, slot_token, slot_route))
    outcome = outcome.reshape(EXPERTS, devices, CAP, D)
    d_inputs = d_inputs.reshape(EXPERTS, devices, CAP, D)
    out_route = outcome[targets, source_dev, position].astype(jnp.float32).reshape(TOKENS, TOP, D)
    mixed = jnp.sum(route_weight[..., None] * out_route, 1).astype(jnp.bfloat16)
    grad_route = jnp.sum(cotangent.astype(jnp.float32)[:, None, :] * out_route, -1)
    back_route = d_inputs[targets, source_dev, position].astype(jnp.float32).reshape(TOKENS, TOP, D)
    grad_tokens = jnp.sum(back_route, 1).astype(jnp.bfloat16)
    return mixed, grad_tokens, grad_route, grad_gate, grad_up, grad_down
```

```python
import functools
import jax
import jax.numpy as jnp
from jax import lax
from jax.experimental import pallas as pl
from jax.experimental.pallas import tpu as pltpu
from jax.sharding import PartitionSpec as P

BF16 = jnp.bfloat16
F32 = jnp.float32
LAST_LAST = (((1,), (1,)), ((), ()))
FIRST_FIRST = (((0,), (0,)), ((), ()))
VMEM_LIMIT = 56 * 1024 * 1024


def iota(shape, dim):
    return lax.broadcasted_iota(jnp.int32, shape, dim)


def dot(a, b, dims=(((1,), (0,)), ((), ()))):
    return lax.dot_general(a, b, dims, preferred_element_type=F32)


def route_slots(ids, placement, cap):
    top, tokens = ids.shape
    experts = placement.shape[1]
    expert = iota((experts, tokens), 0)
    hits = [ids[k : k + 1, :] == expert for k in range(top)]
    named = functools.reduce(jnp.logical_or, hits)
    earlier = (iota((tokens, tokens), 0) < iota((tokens, tokens), 1)).astype(F32)
    count = dot(named.astype(F32).astype(BF16), earlier.astype(BF16)).astype(jnp.int32)
    diagonal = iota((experts, experts), 0) == iota((experts, experts), 1)
    serving = jnp.sum(jnp.where(diagonal, placement, 0), 1, keepdims=True)
    slot = serving * cap + count
    return jnp.concatenate(
        [jnp.sum(jnp.where(hit, slot, 0), 0, keepdims=True) for hit in hits], 0
    )


def selectors(slots, weights, first, rows):
    top, tokens = slots.shape
    row = iota((rows, tokens), 0) + first
    hits = [row == slots[k : k + 1, :] for k in range(top)]
    chosen = functools.reduce(jnp.logical_or, hits)
    weight = functools.reduce(
        jnp.add, [jnp.where(hits[k], weights[k : k + 1, :], 0.0) for k in range(top)]
    )
    high = weight.astype(BF16)
    low = (weight - high.astype(F32)).astype(BF16)
    return hits, chosen.astype(F32).astype(BF16), high, low


def pack_kernel(cap, ids_ref, placement_ref, weight_ref, tokens_ref, cot_ref, out_ref, slots_ref):
    rows = out_ref.shape[0]
    width = tokens_ref.shape[1]

    @pl.when(pl.program_id(0) == 0)
    def _():
        slots_ref[...] = route_slots(ids_ref[...], placement_ref[...], cap)

    _, chosen, high, low = selectors(
        slots_ref[...], weight_ref[...], pl.program_id(0) * rows, rows
    )
    out_ref[:, :width] = dot(chosen, tokens_ref[...]).astype(BF16)
    cot = cot_ref[...]
    out_ref[:, width:] = (dot(high, cot) + dot(low, cot)).astype(BF16)


def pack(ids, placement, weights, tokens, cotangent, cap):
    top, tok_dev = ids.shape
    experts = placement.shape[1]
    width = tokens.shape[1]
    total = experts * cap
    block = min(total, 256)
    whole = lambda shape: pl.BlockSpec(shape, lambda i: (0, 0))
    return pl.pallas_call(
        functools.partial(pack_kernel, cap),
        grid=(total // block,),
        in_specs=[
            whole((top, tok_dev)),
            whole((1, experts)),
            whole((top, tok_dev)),
            whole((tok_dev, width)),
            whole((tok_dev, width)),
        ],
        out_specs=[
            pl.BlockSpec((block, 2 * width), lambda i: (i, 0)),
            whole((top, tok_dev)),
        ],
        out_shape=[
            jax.ShapeDtypeStruct((total, 2 * width), BF16),
            jax.ShapeDtypeStruct((top, tok_dev), jnp.int32),
        ],
        compiler_params=pltpu.CompilerParams(vmem_limit_bytes=VMEM_LIMIT),
        name="pack",
    )(ids, placement, weights, tokens, cotangent)


def expert_kernel(rows_ref, gate_ref, up_ref, down_ref, back_ref, hidden_ref, dgate_ref, dup_ref):
    width = gate_ref.shape[0]
    inputs = rows_ref[:, :width]
    gate_pre = dot(inputs, gate_ref[...])
    up_proj = dot(inputs, up_ref[...])
    sig = jax.nn.sigmoid(gate_pre)
    silu = gate_pre * sig
    hidden = (silu * up_proj).astype(BF16)
    hidden_ref[...] = hidden
    back_ref[:, :width] = dot(hidden, down_ref[...]).astype(BF16)
    d_hidden = dot(rows_ref[:, width:], down_ref[...], LAST_LAST)
    d_gate = (d_hidden * up_proj * sig * (1.0 + gate_pre * (1.0 - sig))).astype(BF16)
    d_up = (d_hidden * silu).astype(BF16)
    dgate_ref[...] = d_gate
    dup_ref[...] = d_up
    back_ref[:, width:] = (
        dot(d_gate, gate_ref[...], LAST_LAST) + dot(d_up, up_ref[...], LAST_LAST)
    ).astype(BF16)


def expert(rows, w_gate, w_up, w_down):
    total, double = rows.shape
    width, hidden = w_gate.shape
    block = min(total, 256)
    strip = lambda n: pl.BlockSpec((block, n), lambda i: (i, 0))
    resident = pl.BlockSpec(memory_space=pltpu.VMEM)
    return pl.pallas_call(
        expert_kernel,
        grid=(total // block,),
        in_specs=[strip(double), resident, resident, resident],
        out_specs=[strip(double), strip(hidden), strip(hidden), strip(hidden)],
        out_shape=[jax.ShapeDtypeStruct((total, double), BF16)]
        + [jax.ShapeDtypeStruct((total, hidden), BF16)] * 3,
        compiler_params=pltpu.CompilerParams(vmem_limit_bytes=VMEM_LIMIT),
        cost_estimate=pl.CostEstimate(
            flops=12 * total * width * hidden, bytes_accessed=2 * total * double * 2, transcendentals=0
        ),
        name="expert",
    )(rows, w_gate, w_up, w_down)


def unpack_kernel(slots_ref, weight_ref, cot_ref, out_ref, din_ref, mixed_ref, gtok_ref, groute_ref, sel_ref, dots_ref):
    step = pl.program_id(0)
    total = out_ref.shape[0]
    tok_dev = cot_ref.shape[0]
    top = slots_ref.shape[0]

    @pl.when(step == 0)
    def _():
        _, chosen, high, low = selectors(slots_ref[...], weight_ref[...], 0, total)
        sel_ref[:, :tok_dev] = high
        sel_ref[:, tok_dev : 2 * tok_dev] = low
        sel_ref[:, 2 * tok_dev :] = chosen
        dots_ref[...] = jnp.zeros_like(dots_ref)

    outcome = out_ref[...]
    halves = dot(sel_ref[:, : 2 * tok_dev], outcome, FIRST_FIRST)
    mixed_ref[...] = (halves[:tok_dev] + halves[tok_dev:]).astype(BF16)
    gtok_ref[...] = dot(sel_ref[:, 2 * tok_dev :], din_ref[...], FIRST_FIRST).astype(BF16)
    dots_ref[...] += dot(outcome, cot_ref[...], LAST_LAST)

    @pl.when(step == pl.num_programs(0) - 1)
    def _():
        slots = slots_ref[...]
        row = iota((total, tok_dev), 0)
        dots = dots_ref[...]
        groute_ref[...] = jnp.concatenate(
            [
                jnp.sum(jnp.where(row == slots[k : k + 1, :], dots, 0.0), 0, keepdims=True)
                for k in range(top)
            ],
            0,
        )


def unpack(slots, weights, cotangent, returned):
    top, tok_dev = slots.shape
    width = cotangent.shape[1]
    total = returned.shape[0]
    block = min(width, 512)
    steps = width // block
    whole = lambda shape: pl.BlockSpec(shape, lambda i: (0, 0))
    return pl.pallas_call(
        unpack_kernel,
        grid=(steps,),
        in_specs=[
            whole((top, tok_dev)),
            whole((top, tok_dev)),
            pl.BlockSpec((tok_dev, block), lambda i: (0, i)),
            pl.BlockSpec((total, block), lambda i: (0, i)),
            pl.BlockSpec((total, block), lambda i: (0, i + steps)),
        ],
        out_specs=[
            pl.BlockSpec((tok_dev, block), lambda i: (0, i)),
            pl.BlockSpec((tok_dev, block), lambda i: (0, i)),
            whole((top, tok_dev)),
        ],
        out_shape=[
            jax.ShapeDtypeStruct((tok_dev, width), BF16),
            jax.ShapeDtypeStruct((tok_dev, width), BF16),
            jax.ShapeDtypeStruct((top, tok_dev), F32),
        ],
        scratch_shapes=[
            pltpu.VMEM((total, 3 * tok_dev), BF16),
            pltpu.VMEM((total, tok_dev), F32),
        ],
        compiler_params=pltpu.CompilerParams(vmem_limit_bytes=VMEM_LIMIT),
        name="unpack",
    )(slots, weights, cotangent, returned, returned)


def exchange(buffer, experts):
    total, width = buffer.shape
    moved = lax.all_to_all(
        buffer.reshape(experts, total // experts, width),
        ("col", "row"),
        split_axis=0,
        concat_axis=0,
        tiled=True,
    )
    return moved.reshape(total, width)


def per_device(tokens, route_weight, expert_ids, placement, w_gate, w_up, w_down, cotangent):
    tok_dev, width = tokens.shape
    fan_out = expert_ids.shape[1]
    experts = placement.shape[0]
    cap = max(2, min(tok_dev // 2, 8 * max(1, tok_dev * fan_out // (8 * experts))))
    weights = route_weight.T
    packed, slots = pack(
        expert_ids.T, placement.reshape(1, experts), weights, tokens, cotangent, cap
    )
    received = exchange(packed, experts)
    back, hidden, d_gate, d_up = expert(received, w_gate[0], w_up[0], w_down[0])
    returned = exchange(back, experts)
    inputs = received[:, :width]
    scaled = received[:, width:]
    grad_gate = dot(inputs, d_gate, FIRST_FIRST).astype(BF16)
    grad_up = dot(inputs, d_up, FIRST_FIRST).astype(BF16)
    grad_down = dot(hidden, scaled, FIRST_FIRST).astype(BF16)
    mixed, grad_tokens, grad_route = unpack(slots, weights, cotangent, returned)
    return (mixed, grad_tokens, grad_route.T, grad_gate[None], grad_up[None], grad_down[None])


def solution(mesh):
    split = P(("col", "row"), None)
    split3 = P(("col", "row"), None, None)
    return jax.shard_map(
        per_device,
        mesh=mesh,
        in_specs=(split, split, split, P(), split3, split3, split3, split),
        out_specs=(split, split, split, split3, split3, split3),
        check_vma=False,
    )
```

```python
import functools
import jax
import jax.numpy as jnp
from jax import lax
from jax.experimental import pallas as pl
from jax.experimental.pallas import tpu as pltpu
from jax.sharding import PartitionSpec as P

BF16 = jnp.bfloat16
F32 = jnp.float32
LAST_LAST = (((1,), (1,)), ((), ()))
FIRST_FIRST = (((0,), (0,)), ((), ()))
VMEM_LIMIT = 56 * 1024 * 1024


def iota(shape, dim):
    return lax.broadcasted_iota(jnp.int32, shape, dim)


def dot(a, b, dims=(((1,), (0,)), ((), ()))):
    return lax.dot_general(a, b, dims, preferred_element_type=F32)


def route_slots(ids, placement, cap):
    top, tokens = ids.shape
    experts = placement.shape[1]
    expert = iota((experts, tokens), 0)
    hits = [ids[k : k + 1, :] == expert for k in range(top)]
    named = functools.reduce(jnp.logical_or, hits)
    earlier = (iota((tokens, tokens), 0) < iota((tokens, tokens), 1)).astype(F32)
    count = dot(named.astype(F32).astype(BF16), earlier.astype(BF16)).astype(jnp.int32)
    diagonal = iota((experts, experts), 0) == iota((experts, experts), 1)
    serving = jnp.sum(jnp.where(diagonal, placement, 0), 1, keepdims=True)
    slot = serving * cap + count
    return jnp.concatenate(
        [jnp.sum(jnp.where(hit, slot, 0), 0, keepdims=True) for hit in hits], 0
    )


def selectors(slots, weights, first, rows):
    top, tokens = slots.shape
    row = iota((rows, tokens), 0) + first
    hits = [row == slots[k : k + 1, :] for k in range(top)]
    chosen = functools.reduce(jnp.logical_or, hits)
    weight = functools.reduce(
        jnp.add, [jnp.where(hits[k], weights[k : k + 1, :], 0.0) for k in range(top)]
    )
    high = weight.astype(BF16)
    low = (weight - high.astype(F32)).astype(BF16)
    return hits, chosen.astype(F32).astype(BF16), high, low


def slots_kernel(cap, ids_ref, placement_ref, weight_ref, tokens_ref, out_ref, slots_ref):
    rows = out_ref.shape[0]

    @pl.when(pl.program_id(0) == 0)
    def _():
        slots_ref[...] = route_slots(ids_ref[...], placement_ref[...], cap)

    _, chosen, _, _ = selectors(slots_ref[...], weight_ref[...], pl.program_id(0) * rows, rows)
    out_ref[...] = dot(chosen, tokens_ref[...]).astype(BF16)


def scaled_kernel(slots_ref, weight_ref, cot_ref, out_ref):
    rows = out_ref.shape[0]
    _, _, high, low = selectors(slots_ref[...], weight_ref[...], pl.program_id(0) * rows, rows)
    cot = cot_ref[...]
    out_ref[...] = (dot(high, cot) + dot(low, cot)).astype(BF16)


def whole(shape):
    return pl.BlockSpec(shape, lambda i: (0, 0))


def strip(block, width):
    return pl.BlockSpec((block, width), lambda i: (i, 0))


def columns(rows, block):
    return pl.BlockSpec((rows, block), lambda i: (0, i))


def params(limit=VMEM_LIMIT):
    return pltpu.CompilerParams(vmem_limit_bytes=limit)


def cost(flops, moved):
    return pl.CostEstimate(flops=flops, bytes_accessed=moved, transcendentals=0)


def pack_tokens(ids, placement, weights, tokens, cap):
    top, tok_dev = ids.shape
    experts = placement.shape[1]
    width = tokens.shape[1]
    total = experts * cap
    block = min(total, 256)
    return pl.pallas_call(
        functools.partial(slots_kernel, cap),
        grid=(total // block,),
        in_specs=[
            whole((top, tok_dev)),
            whole((1, experts)),
            whole((top, tok_dev)),
            whole((tok_dev, width)),
        ],
        out_specs=[strip(block, width), whole((top, tok_dev))],
        out_shape=[
            jax.ShapeDtypeStruct((total, width), BF16),
            jax.ShapeDtypeStruct((top, tok_dev), jnp.int32),
        ],
        compiler_params=params(),
        name="pack_tokens",
    )(ids, placement, weights, tokens)


def pack_scaled(slots, weights, cotangent, total):
    top, tok_dev = slots.shape
    width = cotangent.shape[1]
    block = min(total, 256)
    return pl.pallas_call(
        scaled_kernel,
        grid=(total // block,),
        in_specs=[whole((top, tok_dev)), whole((top, tok_dev)), whole((tok_dev, width))],
        out_specs=strip(block, width),
        out_shape=jax.ShapeDtypeStruct((total, width), BF16),
        compiler_params=params(),
        cost_estimate=cost(4 * total * tok_dev * width, 2 * total * width),
        name="pack_scaled",
    )(slots, weights, cotangent)


def forward_kernel(rows_ref, gate_ref, up_ref, down_ref, out_ref, gate_pre_ref, up_proj_ref, hidden_ref):
    inputs = rows_ref[...]
    gate_pre = dot(inputs, gate_ref[...])
    up_proj = dot(inputs, up_ref[...])
    gate_pre_ref[...] = gate_pre
    up_proj_ref[...] = up_proj
    hidden = (gate_pre * jax.nn.sigmoid(gate_pre) * up_proj).astype(BF16)
    hidden_ref[...] = hidden
    out_ref[...] = dot(hidden, down_ref[...]).astype(BF16)


def forward(rows, w_gate, w_up, w_down):
    total, width = rows.shape
    ff = w_gate.shape[1]
    block = min(total, 256)
    return pl.pallas_call(
        forward_kernel,
        grid=(total // block,),
        in_specs=[strip(block, width)] + [pl.BlockSpec(memory_space=pltpu.VMEM)] * 3,
        out_specs=[strip(block, width), strip(block, ff), strip(block, ff), strip(block, ff)],
        out_shape=[
            jax.ShapeDtypeStruct((total, width), BF16),
            jax.ShapeDtypeStruct((total, ff), F32),
            jax.ShapeDtypeStruct((total, ff), F32),
            jax.ShapeDtypeStruct((total, ff), BF16),
        ],
        compiler_params=params(),
        cost_estimate=cost(6 * total * width * ff, 4 * total * width + 6 * width * ff + 10 * total * ff),
        name="expert_forward",
    )(rows, w_gate, w_up, w_down)


def backward_kernel(rows_ref, gate_pre_ref, up_proj_ref, gate_ref, up_ref, down_ref, din_ref, dgate_ref, dup_ref):
    d_hidden = dot(rows_ref[...], down_ref[...], LAST_LAST)
    gate_pre = gate_pre_ref[...]
    sig = jax.nn.sigmoid(gate_pre)
    d_gate = (d_hidden * up_proj_ref[...] * sig * (1.0 + gate_pre * (1.0 - sig))).astype(BF16)
    d_up = (d_hidden * gate_pre * sig).astype(BF16)
    dgate_ref[...] = d_gate
    dup_ref[...] = d_up
    din_ref[...] = (
        dot(d_gate, gate_ref[...], LAST_LAST) + dot(d_up, up_ref[...], LAST_LAST)
    ).astype(BF16)


def backward(rows, gate_pre, up_proj, w_gate, w_up, w_down):
    total, width = rows.shape
    ff = w_gate.shape[1]
    block = min(total, 256)
    return pl.pallas_call(
        backward_kernel,
        grid=(total // block,),
        in_specs=[strip(block, width), strip(block, ff), strip(block, ff)]
        + [pl.BlockSpec(memory_space=pltpu.VMEM)] * 3,
        out_specs=[strip(block, width), strip(block, ff), strip(block, ff)],
        out_shape=[
            jax.ShapeDtypeStruct((total, width), BF16),
            jax.ShapeDtypeStruct((total, ff), BF16),
            jax.ShapeDtypeStruct((total, ff), BF16),
        ],
        compiler_params=params(),
        cost_estimate=cost(6 * total * width * ff, 4 * total * width + 6 * width * ff + 12 * total * ff),
        name="expert_backward",
    )(rows, gate_pre, up_proj, w_gate, w_up, w_down)


def mixed_kernel(slots_ref, weight_ref, cot_ref, out_ref, mixed_ref, groute_ref, sel_ref, dots_ref):
    step = pl.program_id(0)
    total = out_ref.shape[0]
    tok_dev = cot_ref.shape[0]
    top = slots_ref.shape[0]

    @pl.when(step == 0)
    def _():
        _, _, high, low = selectors(slots_ref[...], weight_ref[...], 0, total)
        sel_ref[:, :tok_dev] = high
        sel_ref[:, tok_dev:] = low
        dots_ref[...] = jnp.zeros_like(dots_ref)

    outcome = out_ref[...]
    halves = dot(sel_ref[...], outcome, FIRST_FIRST)
    mixed_ref[...] = (halves[:tok_dev] + halves[tok_dev:]).astype(BF16)
    dots_ref[...] += dot(outcome, cot_ref[...], LAST_LAST)

    @pl.when(step == pl.num_programs(0) - 1)
    def _():
        slots = slots_ref[...]
        row = iota((total, tok_dev), 0)
        dots = dots_ref[...]
        groute_ref[...] = jnp.concatenate(
            [
                jnp.sum(jnp.where(row == slots[k : k + 1, :], dots, 0.0), 0, keepdims=True)
                for k in range(top)
            ],
            0,
        )


def unpack_mixed(slots, weights, cotangent, outcome):
    top, tok_dev = slots.shape
    total, width = outcome.shape
    block = min(width, 512)
    return pl.pallas_call(
        mixed_kernel,
        grid=(width // block,),
        in_specs=[
            whole((top, tok_dev)),
            whole((top, tok_dev)),
            columns(tok_dev, block),
            columns(total, block),
        ],
        out_specs=[columns(tok_dev, block), whole((top, tok_dev))],
        out_shape=[
            jax.ShapeDtypeStruct((tok_dev, width), BF16),
            jax.ShapeDtypeStruct((top, tok_dev), F32),
        ],
        scratch_shapes=[
            pltpu.VMEM((total, 2 * tok_dev), BF16),
            pltpu.VMEM((total, tok_dev), F32),
        ],
        compiler_params=params(),
        cost_estimate=cost(6 * total * tok_dev * width, 2 * total * width),
        name="unpack_mixed",
    )(slots, weights, cotangent, outcome)


def gtok_kernel(slots_ref, din_ref, gtok_ref, sel_ref):
    total = din_ref.shape[0]

    @pl.when(pl.program_id(0) == 0)
    def _():
        slots = slots_ref[...]
        row = iota((total, slots.shape[1]), 0)
        hits = [row == slots[k : k + 1, :] for k in range(slots.shape[0])]
        sel_ref[...] = functools.reduce(jnp.logical_or, hits).astype(F32).astype(BF16)

    gtok_ref[...] = dot(sel_ref[...], din_ref[...], FIRST_FIRST).astype(BF16)


def unpack_tokens(slots, d_inputs):
    top, tok_dev = slots.shape
    total, width = d_inputs.shape
    block = min(width, 512)
    return pl.pallas_call(
        gtok_kernel,
        grid=(width // block,),
        in_specs=[whole((top, tok_dev)), columns(total, block)],
        out_specs=columns(tok_dev, block),
        out_shape=jax.ShapeDtypeStruct((tok_dev, width), BF16),
        scratch_shapes=[pltpu.VMEM((total, tok_dev), BF16)],
        compiler_params=params(),
        cost_estimate=cost(2 * total * tok_dev * width, 2 * total * width),
        name="unpack_tokens",
    )(slots, d_inputs)


def exchange(buffer, experts):
    total, width = buffer.shape
    moved = lax.all_to_all(
        buffer.reshape(experts, total // experts, width),
        ("col", "row"),
        split_axis=0,
        concat_axis=0,
        tiled=True,
    )
    return moved.reshape(total, width)


def per_device(tokens, route_weight, expert_ids, placement, w_gate, w_up, w_down, cotangent):
    tok_dev, width = tokens.shape
    fan_out = expert_ids.shape[1]
    experts = placement.shape[0]
    cap = max(2, min(tok_dev // 2, 8 * max(1, tok_dev * fan_out // (8 * experts))))
    weights = route_weight.T
    gate, up, down = w_gate[0], w_up[0], w_down[0]
    packed, slots = pack_tokens(
        expert_ids.T, placement.reshape(1, experts), weights, tokens, cap
    )
    inputs = exchange(packed, experts)
    scaled = exchange(pack_scaled(slots, weights, cotangent, experts * cap), experts)
    outcome, gate_pre, up_proj, hidden = forward(inputs, gate, up, down)
    outcome = exchange(outcome, experts)
    d_inputs, d_gate, d_up = backward(scaled, gate_pre, up_proj, gate, up, down)
    returned = exchange(d_inputs, experts)
    grad_gate = dot(inputs, d_gate, FIRST_FIRST).astype(BF16)
    grad_up = dot(inputs, d_up, FIRST_FIRST).astype(BF16)
    grad_down = dot(hidden, scaled, FIRST_FIRST).astype(BF16)
    mixed, grad_route = unpack_mixed(slots, weights, cotangent, outcome)
    grad_tokens = unpack_tokens(slots, returned)
    return (mixed, grad_tokens, grad_route.T, grad_gate[None], grad_up[None], grad_down[None])


def solution(mesh):
    split = P(("col", "row"), None)
    split3 = P(("col", "row"), None, None)
    return jax.shard_map(
        per_device,
        mesh=mesh,
        in_specs=(split, split, split, P(), split3, split3, split3, split),
        out_specs=(split, split, split, split3, split3, split3),
        check_vma=False,
    )
```

```python
import functools
import jax
import jax.numpy as jnp
from jax import lax
from jax.experimental import pallas as pl
from jax.experimental.pallas import tpu as pltpu
from jax.sharding import PartitionSpec as P

BF16 = jnp.bfloat16
F32 = jnp.float32
LAST_LAST = (((1,), (1,)), ((), ()))
FIRST_FIRST = (((0,), (0,)), ((), ()))
VMEM_LIMIT = 56 * 1024 * 1024
PACK_CHUNKS = 4
UNPACK_CHUNKS = 4


def iota(shape, dim):
    return lax.broadcasted_iota(jnp.int32, shape, dim)


def dot(a, b, dims=(((1,), (0,)), ((), ()))):
    return lax.dot_general(a, b, dims, preferred_element_type=F32)


def route_slots(ids, placement, cap):
    top, tokens = ids.shape
    experts = placement.shape[1]
    expert = iota((experts, tokens), 0)
    hits = [ids[k : k + 1, :] == expert for k in range(top)]
    named = functools.reduce(jnp.logical_or, hits)
    earlier = (iota((tokens, tokens), 0) < iota((tokens, tokens), 1)).astype(F32)
    count = dot(named.astype(F32).astype(BF16), earlier.astype(BF16)).astype(jnp.int32)
    diagonal = iota((experts, experts), 0) == iota((experts, experts), 1)
    serving = jnp.sum(jnp.where(diagonal, placement, 0), 1, keepdims=True)
    slot = serving * cap + count
    return jnp.concatenate(
        [jnp.sum(jnp.where(hit, slot, 0), 0, keepdims=True) for hit in hits], 0
    )


def hits_of(slots, first, rows):
    row = iota((rows, slots.shape[1]), 0) + first
    hits = [row == slots[k : k + 1, :] for k in range(slots.shape[0])]
    return jnp.where(functools.reduce(jnp.logical_or, hits), 1.0, 0.0).astype(BF16)


def selectors(slots, weights, first, rows):
    top, tokens = slots.shape
    row = iota((rows, tokens), 0) + first
    hits = [row == slots[k : k + 1, :] for k in range(top)]
    chosen = functools.reduce(jnp.logical_or, hits)
    weight = functools.reduce(
        jnp.add, [jnp.where(hits[k], weights[k : k + 1, :], 0.0) for k in range(top)]
    )
    high = weight.astype(BF16)
    low = (weight - high.astype(F32)).astype(BF16)
    return hits, chosen.astype(F32).astype(BF16), high, low


def slots_kernel(cap, chunks, ids_ref, placement_ref, tokens_ref, out_ref, slots_ref, rows_ref, sems):
    size = rows_ref.shape[1]
    slots = route_slots(ids_ref[...], placement_ref[...], cap)
    slots_ref[...] = slots
    copies = []
    for i in range(chunks):
        chosen = hits_of(slots, i * size, size)
        rows_ref[i] = dot(chosen, tokens_ref[...]).astype(BF16)
        copies.append(
            pltpu.make_async_copy(rows_ref.at[i], out_ref.at[pl.ds(i * size, size)], sems.at[i])
        )
        copies[-1].start()
    for copy in copies:
        copy.wait()


def scaled_kernel(slots_ref, weight_ref, cot_ref, out_ref):
    rows = out_ref.shape[0]
    _, _, high, low = selectors(slots_ref[...], weight_ref[...], pl.program_id(0) * rows, rows)
    cot = cot_ref[...]
    out_ref[...] = (dot(high, cot) + dot(low, cot)).astype(BF16)


def whole(shape):
    return pl.BlockSpec(shape, lambda i: (0, 0))


def strip(block, width):
    return pl.BlockSpec((block, width), lambda i: (i, 0))


def columns(rows, block):
    return pl.BlockSpec((rows, block), lambda i: (0, i))


def params(limit=VMEM_LIMIT):
    return pltpu.CompilerParams(vmem_limit_bytes=limit)


def cost(flops, moved):
    return pl.CostEstimate(flops=flops, bytes_accessed=moved, transcendentals=0)


def pack_tokens(ids, placement, tokens, cap, chunks=PACK_CHUNKS):
    top, tok_dev = ids.shape
    experts = placement.shape[1]
    width = tokens.shape[1]
    total = experts * cap
    in_vmem = pl.BlockSpec(memory_space=pltpu.VMEM)
    return pl.pallas_call(
        functools.partial(slots_kernel, cap, chunks),
        in_specs=[in_vmem] * 3,
        out_specs=[pl.BlockSpec(memory_space=pl.ANY), in_vmem],
        out_shape=[
            jax.ShapeDtypeStruct((total, width), BF16),
            jax.ShapeDtypeStruct((top, tok_dev), jnp.int32),
        ],
        scratch_shapes=[
            pltpu.VMEM((chunks, total // chunks, width), BF16),
            pltpu.SemaphoreType.DMA((chunks,)),
        ],
        compiler_params=params(),
        name="pack_tokens",
    )(ids, placement, tokens)


def pack_scaled(slots, weights, cotangent, total):
    top, tok_dev = slots.shape
    width = cotangent.shape[1]
    block = min(total, 256)
    return pl.pallas_call(
        scaled_kernel,
        grid=(total // block,),
        in_specs=[whole((top, tok_dev)), whole((top, tok_dev)), whole((tok_dev, width))],
        out_specs=strip(block, width),
        out_shape=jax.ShapeDtypeStruct((total, width), BF16),
        compiler_params=params(),
        cost_estimate=cost(4 * total * tok_dev * width, 2 * total * width),
        name="pack_scaled",
    )(slots, weights, cotangent)


def forward_kernel(rows_ref, gate_ref, up_ref, down_ref, out_ref, gate_pre_ref, up_proj_ref, hidden_ref):
    inputs = rows_ref[...]
    gate_pre = dot(inputs, gate_ref[...])
    up_proj = dot(inputs, up_ref[...])
    gate_pre_ref[...] = gate_pre
    up_proj_ref[...] = up_proj
    hidden = (gate_pre * jax.nn.sigmoid(gate_pre) * up_proj).astype(BF16)
    hidden_ref[...] = hidden
    out_ref[...] = dot(hidden, down_ref[...]).astype(BF16)


def forward(rows, w_gate, w_up, w_down):
    total, width = rows.shape
    ff = w_gate.shape[1]
    block = min(total, 256)
    return pl.pallas_call(
        forward_kernel,
        grid=(total // block,),
        in_specs=[strip(block, width)] + [pl.BlockSpec(memory_space=pltpu.VMEM)] * 3,
        out_specs=[strip(block, width), strip(block, ff), strip(block, ff), strip(block, ff)],
        out_shape=[
            jax.ShapeDtypeStruct((total, width), BF16),
            jax.ShapeDtypeStruct((total, ff), F32),
            jax.ShapeDtypeStruct((total, ff), F32),
            jax.ShapeDtypeStruct((total, ff), BF16),
        ],
        compiler_params=params(),
        cost_estimate=cost(6 * total * width * ff, 4 * total * width + 6 * width * ff + 10 * total * ff),
        name="expert_forward",
    )(rows, w_gate, w_up, w_down)


def backward_kernel(rows_ref, gate_pre_ref, up_proj_ref, gate_ref, up_ref, down_ref, din_ref, dgate_ref, dup_ref):
    d_hidden = dot(rows_ref[...], down_ref[...], LAST_LAST)
    gate_pre = gate_pre_ref[...]
    sig = jax.nn.sigmoid(gate_pre)
    d_gate = (d_hidden * up_proj_ref[...] * sig * (1.0 + gate_pre * (1.0 - sig))).astype(BF16)
    d_up = (d_hidden * gate_pre * sig).astype(BF16)
    dgate_ref[...] = d_gate
    dup_ref[...] = d_up
    din_ref[...] = (
        dot(d_gate, gate_ref[...], LAST_LAST) + dot(d_up, up_ref[...], LAST_LAST)
    ).astype(BF16)


def backward(rows, gate_pre, up_proj, w_gate, w_up, w_down):
    total, width = rows.shape
    ff = w_gate.shape[1]
    block = min(total, 256)
    return pl.pallas_call(
        backward_kernel,
        grid=(total // block,),
        in_specs=[strip(block, width), strip(block, ff), strip(block, ff)]
        + [pl.BlockSpec(memory_space=pltpu.VMEM)] * 3,
        out_specs=[strip(block, width), strip(block, ff), strip(block, ff)],
        out_shape=[
            jax.ShapeDtypeStruct((total, width), BF16),
            jax.ShapeDtypeStruct((total, ff), BF16),
            jax.ShapeDtypeStruct((total, ff), BF16),
        ],
        compiler_params=params(),
        cost_estimate=cost(6 * total * width * ff, 4 * total * width + 6 * width * ff + 12 * total * ff),
        name="expert_backward",
    )(rows, gate_pre, up_proj, w_gate, w_up, w_down)


def mixed_kernel(slots_ref, weight_ref, cot_ref, out_ref, mixed_ref, groute_ref, sel_ref, dots_ref):
    step = pl.program_id(0)
    total = out_ref.shape[0]
    tok_dev = cot_ref.shape[0]
    top = slots_ref.shape[0]

    @pl.when(step == 0)
    def _():
        _, _, high, low = selectors(slots_ref[...], weight_ref[...], 0, total)
        sel_ref[:, :tok_dev] = high
        sel_ref[:, tok_dev:] = low
        dots_ref[...] = jnp.zeros_like(dots_ref)

    outcome = out_ref[...]
    halves = dot(sel_ref[...], outcome, FIRST_FIRST)
    mixed_ref[...] = (halves[:tok_dev] + halves[tok_dev:]).astype(BF16)
    dots_ref[...] += dot(outcome, cot_ref[...], LAST_LAST)

    @pl.when(step == pl.num_programs(0) - 1)
    def _():
        slots = slots_ref[...]
        row = iota((total, tok_dev), 0)
        dots = dots_ref[...]
        groute_ref[...] = jnp.concatenate(
            [
                jnp.sum(jnp.where(row == slots[k : k + 1, :], dots, 0.0), 0, keepdims=True)
                for k in range(top)
            ],
            0,
        )


def unpack_mixed(slots, weights, cotangent, outcome):
    top, tok_dev = slots.shape
    total, width = outcome.shape
    block = min(width, 512)
    return pl.pallas_call(
        mixed_kernel,
        grid=(width // block,),
        in_specs=[
            whole((top, tok_dev)),
            whole((top, tok_dev)),
            columns(tok_dev, block),
            columns(total, block),
        ],
        out_specs=[columns(tok_dev, block), whole((top, tok_dev))],
        out_shape=[
            jax.ShapeDtypeStruct((tok_dev, width), BF16),
            jax.ShapeDtypeStruct((top, tok_dev), F32),
        ],
        scratch_shapes=[
            pltpu.VMEM((total, 2 * tok_dev), BF16),
            pltpu.VMEM((total, tok_dev), F32),
        ],
        compiler_params=params(),
        cost_estimate=cost(6 * total * tok_dev * width, 2 * total * width),
        name="unpack_mixed",
    )(slots, weights, cotangent, outcome)


def gtok_kernel(chunks, slots_ref, din_ref, gtok_ref, rows_ref, part_ref, in_sems, out_sems):
    total, width = din_ref.shape
    size = width // chunks
    arrivals = []
    for i in range(chunks):
        arrivals.append(
            pltpu.make_async_copy(
                din_ref.at[:, pl.ds(i * size, size)], rows_ref.at[i], in_sems.at[i]
            )
        )
        arrivals[-1].start()
    chosen = hits_of(slots_ref[...], 0, total).T
    leaving = []
    for i in range(chunks):
        arrivals[i].wait()
        part_ref[i] = dot(chosen, rows_ref[i]).astype(BF16)
        leaving.append(
            pltpu.make_async_copy(
                part_ref.at[i], gtok_ref.at[:, pl.ds(i * size, size)], out_sems.at[i]
            )
        )
        leaving[-1].start()
    for copy in leaving:
        copy.wait()


def unpack_tokens(slots, d_inputs, chunks=UNPACK_CHUNKS):
    tok_dev = slots.shape[1]
    total, width = d_inputs.shape
    anywhere = pl.BlockSpec(memory_space=pl.ANY)
    return pl.pallas_call(
        functools.partial(gtok_kernel, chunks),
        in_specs=[pl.BlockSpec(memory_space=pltpu.VMEM), anywhere],
        out_specs=anywhere,
        out_shape=jax.ShapeDtypeStruct((tok_dev, width), BF16),
        scratch_shapes=[
            pltpu.VMEM((chunks, total, width // chunks), BF16),
            pltpu.VMEM((chunks, tok_dev, width // chunks), BF16),
            pltpu.SemaphoreType.DMA((chunks,)),
            pltpu.SemaphoreType.DMA((chunks,)),
        ],
        compiler_params=params(),
        cost_estimate=cost(2 * total * tok_dev * width, 2 * total * width),
        name="unpack_tokens",
    )(slots, d_inputs)


def exchange(buffer, experts):
    total, width = buffer.shape
    moved = lax.all_to_all(
        buffer.reshape(experts, total // experts, width),
        ("col", "row"),
        split_axis=0,
        concat_axis=0,
        tiled=True,
    )
    return moved.reshape(total, width)


def per_device(tokens, route_weight, expert_ids, placement, w_gate, w_up, w_down, cotangent):
    tok_dev, width = tokens.shape
    fan_out = expert_ids.shape[1]
    experts = placement.shape[0]
    cap = max(2, min(tok_dev // 2, 8 * max(1, tok_dev * fan_out // (8 * experts))))
    weights = route_weight.T
    gate, up, down = w_gate[0], w_up[0], w_down[0]
    packed, slots = pack_tokens(
        expert_ids.T, placement.reshape(1, experts), tokens, cap
    )
    inputs = exchange(packed, experts)
    scaled = exchange(pack_scaled(slots, weights, cotangent, experts * cap), experts)
    outcome, gate_pre, up_proj, hidden = forward(inputs, gate, up, down)
    outcome = exchange(outcome, experts)
    d_inputs, d_gate, d_up = backward(scaled, gate_pre, up_proj, gate, up, down)
    returned = exchange(d_inputs, experts)
    grad_gate = dot(inputs, d_gate, FIRST_FIRST).astype(BF16)
    grad_up = dot(inputs, d_up, FIRST_FIRST).astype(BF16)
    grad_down = dot(hidden, scaled, FIRST_FIRST).astype(BF16)
    mixed, grad_route = unpack_mixed(slots, weights, cotangent, outcome)
    grad_tokens = unpack_tokens(slots, returned)
    return (mixed, grad_tokens, grad_route.T, grad_gate[None], grad_up[None], grad_down[None])


def solution(mesh):
    split = P(("col", "row"), None)
    split3 = P(("col", "row"), None, None)
    return jax.shard_map(
        per_device,
        mesh=mesh,
        in_specs=(split, split, split, P(), split3, split3, split3, split),
        out_specs=(split, split, split, split3, split3, split3),
        check_vma=False,
    )
```

```python
import functools
import math
import jax
import jax.numpy as jnp
import numpy as np
from jax import lax
from jax.experimental import pallas as pl
from jax.experimental.pallas import tpu as pltpu
from jax.sharding import PartitionSpec as P

BF16 = jnp.bfloat16
F32 = jnp.float32
LAST_LAST = (((1,), (1,)), ((), ()))
FIRST_FIRST = (((0,), (0,)), ((), ()))
VMEM_LIMIT = 56 * 1024 * 1024
PACK_CHUNKS = 4
UNPACK_CHUNKS = 4


def iota(shape, dim):
    return lax.broadcasted_iota(jnp.int32, shape, dim)


def dot(a, b, dims=(((1,), (0,)), ((), ()))):
    return lax.dot_general(a, b, dims, preferred_element_type=F32)


def send_order(columns_, rows_):
    side = math.isqrt(columns_)
    cores = 2 if rows_ % 2 == 0 else 1
    lines = rows_ // cores
    x = (columns_ // side, side * rows_)
    z = (side, rows_)
    y = (lines, cores)
    core = (cores, 1)
    return (z, core, x, y)


def block_of(number, order):
    block = jnp.zeros_like(number)
    for size, stride in order:
        block = block * size + (number // stride) % size
    return block


def devices_of(order):
    devices = np.zeros((1,), np.int64)
    for size, stride in order:
        devices = (devices[:, None] + np.arange(size) * stride).reshape(-1)
    return [int(device) for device in devices]


def route_slots(ids, placement, cap):
    top, tokens = ids.shape
    experts = placement.shape[1]
    expert = iota((experts, tokens), 0)
    hits = [ids[k : k + 1, :] == expert for k in range(top)]
    named = functools.reduce(jnp.logical_or, hits)
    earlier = (iota((tokens, tokens), 0) < iota((tokens, tokens), 1)).astype(F32)
    count = dot(named.astype(F32).astype(BF16), earlier.astype(BF16)).astype(jnp.int32)
    diagonal = iota((experts, experts), 0) == iota((experts, experts), 1)
    serving = jnp.sum(jnp.where(diagonal, placement, 0), 1, keepdims=True)
    slot = serving * cap + count
    return jnp.concatenate(
        [jnp.sum(jnp.where(hit, slot, 0), 0, keepdims=True) for hit in hits], 0
    )


def hits_of(slots, first, rows):
    row = iota((rows, slots.shape[1]), 0) + first
    hits = [row == slots[k : k + 1, :] for k in range(slots.shape[0])]
    return jnp.where(functools.reduce(jnp.logical_or, hits), 1.0, 0.0).astype(BF16)


def selectors(slots, weights, first, rows):
    top, tokens = slots.shape
    row = iota((rows, tokens), 0) + first
    hits = [row == slots[k : k + 1, :] for k in range(top)]
    chosen = functools.reduce(jnp.logical_or, hits)
    weight = functools.reduce(
        jnp.add, [jnp.where(hits[k], weights[k : k + 1, :], 0.0) for k in range(top)]
    )
    high = weight.astype(BF16)
    low = (weight - high.astype(F32)).astype(BF16)
    return hits, chosen.astype(F32).astype(BF16), high, low


def slots_kernel(cap, chunks, order, ids_ref, placement_ref, tokens_ref, out_ref, slots_ref, rows_ref, sems):
    size = rows_ref.shape[1]
    slots = route_slots(ids_ref[...], block_of(placement_ref[...], order), cap)
    slots_ref[...] = slots
    copies = []
    for i in range(chunks):
        chosen = hits_of(slots, i * size, size)
        rows_ref[i] = dot(chosen, tokens_ref[...]).astype(BF16)
        copies.append(
            pltpu.make_async_copy(rows_ref.at[i], out_ref.at[pl.ds(i * size, size)], sems.at[i])
        )
        copies[-1].start()
    for copy in copies:
        copy.wait()


def scaled_kernel(slots_ref, weight_ref, cot_ref, out_ref):
    rows = out_ref.shape[0]
    _, _, high, low = selectors(slots_ref[...], weight_ref[...], pl.program_id(0) * rows, rows)
    cot = cot_ref[...]
    out_ref[...] = (dot(high, cot) + dot(low, cot)).astype(BF16)


def whole(shape):
    return pl.BlockSpec(shape, lambda i: (0, 0))


def strip(block, width):
    return pl.BlockSpec((block, width), lambda i: (i, 0))


def columns(rows, block):
    return pl.BlockSpec((rows, block), lambda i: (0, i))


def params(limit=VMEM_LIMIT):
    return pltpu.CompilerParams(vmem_limit_bytes=limit)


def cost(flops, moved):
    return pl.CostEstimate(flops=flops, bytes_accessed=moved, transcendentals=0)


def pack_tokens(ids, placement, tokens, cap, order, chunks=PACK_CHUNKS):
    top, tok_dev = ids.shape
    experts = placement.shape[1]
    width = tokens.shape[1]
    total = experts * cap
    in_vmem = pl.BlockSpec(memory_space=pltpu.VMEM)
    return pl.pallas_call(
        functools.partial(slots_kernel, cap, chunks, order),
        in_specs=[in_vmem] * 3,
        out_specs=[pl.BlockSpec(memory_space=pl.ANY), in_vmem],
        out_shape=[
            jax.ShapeDtypeStruct((total, width), BF16),
            jax.ShapeDtypeStruct((top, tok_dev), jnp.int32),
        ],
        scratch_shapes=[
            pltpu.VMEM((chunks, total // chunks, width), BF16),
            pltpu.SemaphoreType.DMA((chunks,)),
        ],
        compiler_params=params(),
        name="pack_tokens",
    )(ids, placement, tokens)


def pack_scaled(slots, weights, cotangent, total):
    top, tok_dev = slots.shape
    width = cotangent.shape[1]
    block = min(total, 256)
    return pl.pallas_call(
        scaled_kernel,
        grid=(total // block,),
        in_specs=[whole((top, tok_dev)), whole((top, tok_dev)), whole((tok_dev, width))],
        out_specs=strip(block, width),
        out_shape=jax.ShapeDtypeStruct((total, width), BF16),
        compiler_params=params(),
        cost_estimate=cost(4 * total * tok_dev * width, 2 * total * width),
        name="pack_scaled",
    )(slots, weights, cotangent)


def forward_kernel(rows_ref, gate_ref, up_ref, down_ref, out_ref, gate_pre_ref, up_proj_ref, hidden_ref):
    inputs = rows_ref[...]
    gate_pre = dot(inputs, gate_ref[...])
    up_proj = dot(inputs, up_ref[...])
    gate_pre_ref[...] = gate_pre
    up_proj_ref[...] = up_proj
    hidden = (gate_pre * jax.nn.sigmoid(gate_pre) * up_proj).astype(BF16)
    hidden_ref[...] = hidden
    out_ref[...] = dot(hidden, down_ref[...]).astype(BF16)


def forward(rows, w_gate, w_up, w_down):
    total, width = rows.shape
    ff = w_gate.shape[1]
    block = min(total, 256)
    return pl.pallas_call(
        forward_kernel,
        grid=(total // block,),
        in_specs=[strip(block, width)] + [pl.BlockSpec(memory_space=pltpu.VMEM)] * 3,
        out_specs=[strip(block, width), strip(block, ff), strip(block, ff), strip(block, ff)],
        out_shape=[
            jax.ShapeDtypeStruct((total, width), BF16),
            jax.ShapeDtypeStruct((total, ff), F32),
            jax.ShapeDtypeStruct((total, ff), F32),
            jax.ShapeDtypeStruct((total, ff), BF16),
        ],
        compiler_params=params(),
        cost_estimate=cost(6 * total * width * ff, 4 * total * width + 6 * width * ff + 10 * total * ff),
        name="expert_forward",
    )(rows, w_gate, w_up, w_down)


def backward_kernel(rows_ref, gate_pre_ref, up_proj_ref, gate_ref, up_ref, down_ref, din_ref, dgate_ref, dup_ref):
    d_hidden = dot(rows_ref[...], down_ref[...], LAST_LAST)
    gate_pre = gate_pre_ref[...]
    sig = jax.nn.sigmoid(gate_pre)
    d_gate = (d_hidden * up_proj_ref[...] * sig * (1.0 + gate_pre * (1.0 - sig))).astype(BF16)
    d_up = (d_hidden * gate_pre * sig).astype(BF16)
    dgate_ref[...] = d_gate
    dup_ref[...] = d_up
    din_ref[...] = (
        dot(d_gate, gate_ref[...], LAST_LAST) + dot(d_up, up_ref[...], LAST_LAST)
    ).astype(BF16)


def backward(rows, gate_pre, up_proj, w_gate, w_up, w_down):
    total, width = rows.shape
    ff = w_gate.shape[1]
    block = min(total, 256)
    return pl.pallas_call(
        backward_kernel,
        grid=(total // block,),
        in_specs=[strip(block, width), strip(block, ff), strip(block, ff)]
        + [pl.BlockSpec(memory_space=pltpu.VMEM)] * 3,
        out_specs=[strip(block, width), strip(block, ff), strip(block, ff)],
        out_shape=[
            jax.ShapeDtypeStruct((total, width), BF16),
            jax.ShapeDtypeStruct((total, ff), BF16),
            jax.ShapeDtypeStruct((total, ff), BF16),
        ],
        compiler_params=params(),
        cost_estimate=cost(6 * total * width * ff, 4 * total * width + 6 * width * ff + 12 * total * ff),
        name="expert_backward",
    )(rows, gate_pre, up_proj, w_gate, w_up, w_down)


def mixed_kernel(slots_ref, weight_ref, cot_ref, out_ref, mixed_ref, groute_ref, sel_ref, dots_ref):
    step = pl.program_id(0)
    total = out_ref.shape[0]
    tok_dev = cot_ref.shape[0]
    top = slots_ref.shape[0]

    @pl.when(step == 0)
    def _():
        _, _, high, low = selectors(slots_ref[...], weight_ref[...], 0, total)
        sel_ref[:, :tok_dev] = high
        sel_ref[:, tok_dev:] = low
        dots_ref[...] = jnp.zeros_like(dots_ref)

    outcome = out_ref[...]
    halves = dot(sel_ref[...], outcome, FIRST_FIRST)
    mixed_ref[...] = (halves[:tok_dev] + halves[tok_dev:]).astype(BF16)
    dots_ref[...] += dot(outcome, cot_ref[...], LAST_LAST)

    @pl.when(step == pl.num_programs(0) - 1)
    def _():
        slots = slots_ref[...]
        row = iota((total, tok_dev), 0)
        dots = dots_ref[...]
        groute_ref[...] = jnp.concatenate(
            [
                jnp.sum(jnp.where(row == slots[k : k + 1, :], dots, 0.0), 0, keepdims=True)
                for k in range(top)
            ],
            0,
        )


def unpack_mixed(slots, weights, cotangent, outcome):
    top, tok_dev = slots.shape
    total, width = outcome.shape
    block = min(width, 512)
    return pl.pallas_call(
        mixed_kernel,
        grid=(width // block,),
        in_specs=[
            whole((top, tok_dev)),
            whole((top, tok_dev)),
            columns(tok_dev, block),
            columns(total, block),
        ],
        out_specs=[columns(tok_dev, block), whole((top, tok_dev))],
        out_shape=[
            jax.ShapeDtypeStruct((tok_dev, width), BF16),
            jax.ShapeDtypeStruct((top, tok_dev), F32),
        ],
        scratch_shapes=[
            pltpu.VMEM((total, 2 * tok_dev), BF16),
            pltpu.VMEM((total, tok_dev), F32),
        ],
        compiler_params=params(),
        cost_estimate=cost(6 * total * tok_dev * width, 2 * total * width),
        name="unpack_mixed",
    )(slots, weights, cotangent, outcome)


def gtok_kernel(chunks, slots_ref, din_ref, gtok_ref, rows_ref, part_ref, in_sems, out_sems):
    total, width = din_ref.shape
    size = width // chunks
    arrivals = []
    for i in range(chunks):
        arrivals.append(
            pltpu.make_async_copy(
                din_ref.at[:, pl.ds(i * size, size)], rows_ref.at[i], in_sems.at[i]
            )
        )
        arrivals[-1].start()
    chosen = hits_of(slots_ref[...], 0, total).T
    leaving = []
    for i in range(chunks):
        arrivals[i].wait()
        part_ref[i] = dot(chosen, rows_ref[i]).astype(BF16)
        leaving.append(
            pltpu.make_async_copy(
                part_ref.at[i], gtok_ref.at[:, pl.ds(i * size, size)], out_sems.at[i]
            )
        )
        leaving[-1].start()
    for copy in leaving:
        copy.wait()


def unpack_tokens(slots, d_inputs, chunks=UNPACK_CHUNKS):
    tok_dev = slots.shape[1]
    total, width = d_inputs.shape
    anywhere = pl.BlockSpec(memory_space=pl.ANY)
    return pl.pallas_call(
        functools.partial(gtok_kernel, chunks),
        in_specs=[pl.BlockSpec(memory_space=pltpu.VMEM), anywhere],
        out_specs=anywhere,
        out_shape=jax.ShapeDtypeStruct((tok_dev, width), BF16),
        scratch_shapes=[
            pltpu.VMEM((chunks, total, width // chunks), BF16),
            pltpu.VMEM((chunks, tok_dev, width // chunks), BF16),
            pltpu.SemaphoreType.DMA((chunks,)),
            pltpu.SemaphoreType.DMA((chunks,)),
        ],
        compiler_params=params(),
        cost_estimate=cost(2 * total * tok_dev * width, 2 * total * width),
        name="unpack_tokens",
    )(slots, d_inputs)


def exchange(buffer, experts, order):
    total, width = buffer.shape
    moved = lax.all_to_all(
        buffer.reshape(experts, total // experts, width),
        ("col", "row"),
        split_axis=0,
        concat_axis=0,
        tiled=True,
        axis_index_groups=[devices_of(order)],
    )
    return moved.reshape(total, width)


def per_device(order, tokens, route_weight, expert_ids, placement, w_gate, w_up, w_down, cotangent):
    tok_dev, width = tokens.shape
    fan_out = expert_ids.shape[1]
    experts = placement.shape[0]
    cap = max(2, min(tok_dev // 2, 8 * max(1, tok_dev * fan_out // (8 * experts))))
    weights = route_weight.T
    gate, up, down = w_gate[0], w_up[0], w_down[0]
    packed, slots = pack_tokens(
        expert_ids.T, placement.reshape(1, experts), tokens, cap, order
    )
    inputs = exchange(packed, experts, order)
    scaled = exchange(pack_scaled(slots, weights, cotangent, experts * cap), experts, order)
    outcome, gate_pre, up_proj, hidden = forward(inputs, gate, up, down)
    outcome = exchange(outcome, experts, order)
    d_inputs, d_gate, d_up = backward(scaled, gate_pre, up_proj, gate, up, down)
    returned = exchange(d_inputs, experts, order)
    grad_gate = dot(inputs, d_gate, FIRST_FIRST).astype(BF16)
    grad_up = dot(inputs, d_up, FIRST_FIRST).astype(BF16)
    grad_down = dot(hidden, scaled, FIRST_FIRST).astype(BF16)
    mixed, grad_route = unpack_mixed(slots, weights, cotangent, outcome)
    grad_tokens = unpack_tokens(slots, returned)
    return (mixed, grad_tokens, grad_route.T, grad_gate[None], grad_up[None], grad_down[None])


def solution(mesh):
    split = P(("col", "row"), None)
    split3 = P(("col", "row"), None, None)
    order = send_order(mesh.shape["col"], mesh.shape["row"])
    return jax.shard_map(
        functools.partial(per_device, order),
        mesh=mesh,
        in_specs=(split, split, split, P(), split3, split3, split3, split),
        out_specs=(split, split, split, split3, split3, split3),
        check_vma=False,
    )
```

```python
import functools
import math
import jax
import jax.numpy as jnp
import numpy as np
from jax import lax
from jax.experimental import pallas as pl
from jax.experimental.pallas import tpu as pltpu
from jax.sharding import PartitionSpec as P

BF16 = jnp.bfloat16
F32 = jnp.float32
LAST_LAST = (((1,), (1,)), ((), ()))
FIRST_FIRST = (((0,), (0,)), ((), ()))
VMEM_LIMIT = 56 * 1024 * 1024
PACK_CHUNKS = 4
UNPACK_CHUNKS = 4


def iota(shape, dim):
    return lax.broadcasted_iota(jnp.int32, shape, dim)


def dot(a, b, dims=(((1,), (0,)), ((), ()))):
    return lax.dot_general(a, b, dims, preferred_element_type=F32)


def send_order(columns_, rows_):
    side = math.isqrt(columns_)
    cores = 2 if rows_ % 2 == 0 else 1
    lines = rows_ // cores
    x = (columns_ // side, side * rows_, False)
    z = (side, rows_, side == 4)
    y = (lines, cores, False)
    core = (cores, 1, False)
    return (z, core, x, y)


def digit_of(value, reflected):
    return value ^ (value >> 1) if reflected else value


def block_of(number, order):
    block = jnp.zeros_like(number)
    for size, stride, reflected in order:
        block = block * size + digit_of((number // stride) % size, reflected)
    return block


def devices_of(order):
    devices = np.zeros((1,), np.int64)
    for size, stride, reflected in order:
        steps = digit_of(np.arange(size), reflected) * stride
        devices = (devices[:, None] + steps).reshape(-1)
    return [int(device) for device in devices]


def route_slots(ids, placement, cap):
    top, tokens = ids.shape
    experts = placement.shape[1]
    expert = iota((experts, tokens), 0)
    hits = [ids[k : k + 1, :] == expert for k in range(top)]
    named = functools.reduce(jnp.logical_or, hits)
    earlier = (iota((tokens, tokens), 0) < iota((tokens, tokens), 1)).astype(F32)
    count = dot(named.astype(F32).astype(BF16), earlier.astype(BF16)).astype(jnp.int32)
    diagonal = iota((experts, experts), 0) == iota((experts, experts), 1)
    serving = jnp.sum(jnp.where(diagonal, placement, 0), 1, keepdims=True)
    slot = serving * cap + count
    return jnp.concatenate(
        [jnp.sum(jnp.where(hit, slot, 0), 0, keepdims=True) for hit in hits], 0
    )


def hits_of(slots, first, rows):
    row = iota((rows, slots.shape[1]), 0) + first
    hits = [row == slots[k : k + 1, :] for k in range(slots.shape[0])]
    return jnp.where(functools.reduce(jnp.logical_or, hits), 1.0, 0.0).astype(BF16)


def selectors(slots, weights, first, rows):
    top, tokens = slots.shape
    row = iota((rows, tokens), 0) + first
    hits = [row == slots[k : k + 1, :] for k in range(top)]
    chosen = functools.reduce(jnp.logical_or, hits)
    weight = functools.reduce(
        jnp.add, [jnp.where(hits[k], weights[k : k + 1, :], 0.0) for k in range(top)]
    )
    high = weight.astype(BF16)
    low = (weight - high.astype(F32)).astype(BF16)
    return hits, chosen.astype(F32).astype(BF16), high, low


def slots_kernel(cap, chunks, order, ids_ref, placement_ref, tokens_ref, out_ref, slots_ref, rows_ref, sems):
    size = rows_ref.shape[1]
    slots = route_slots(ids_ref[...], block_of(placement_ref[...], order), cap)
    slots_ref[...] = slots
    copies = []
    for i in range(chunks):
        chosen = hits_of(slots, i * size, size)
        rows_ref[i] = dot(chosen, tokens_ref[...]).astype(BF16)
        copies.append(
            pltpu.make_async_copy(rows_ref.at[i], out_ref.at[pl.ds(i * size, size)], sems.at[i])
        )
        copies[-1].start()
    for copy in copies:
        copy.wait()


def scaled_kernel(slots_ref, weight_ref, cot_ref, out_ref):
    rows = out_ref.shape[0]
    _, _, high, low = selectors(slots_ref[...], weight_ref[...], pl.program_id(0) * rows, rows)
    cot = cot_ref[...]
    out_ref[...] = (dot(high, cot) + dot(low, cot)).astype(BF16)


def whole(shape):
    return pl.BlockSpec(shape, lambda i: (0, 0))


def strip(block, width):
    return pl.BlockSpec((block, width), lambda i: (i, 0))


def columns(rows, block):
    return pl.BlockSpec((rows, block), lambda i: (0, i))


def params(limit=VMEM_LIMIT):
    return pltpu.CompilerParams(vmem_limit_bytes=limit)


def cost(flops, moved):
    return pl.CostEstimate(flops=flops, bytes_accessed=moved, transcendentals=0)


def pack_tokens(ids, placement, tokens, cap, order, chunks=PACK_CHUNKS):
    top, tok_dev = ids.shape
    experts = placement.shape[1]
    width = tokens.shape[1]
    total = experts * cap
    in_vmem = pl.BlockSpec(memory_space=pltpu.VMEM)
    return pl.pallas_call(
        functools.partial(slots_kernel, cap, chunks, order),
        in_specs=[in_vmem] * 3,
        out_specs=[pl.BlockSpec(memory_space=pl.ANY), in_vmem],
        out_shape=[
            jax.ShapeDtypeStruct((total, width), BF16),
            jax.ShapeDtypeStruct((top, tok_dev), jnp.int32),
        ],
        scratch_shapes=[
            pltpu.VMEM((chunks, total // chunks, width), BF16),
            pltpu.SemaphoreType.DMA((chunks,)),
        ],
        compiler_params=params(),
        name="pack_tokens",
    )(ids, placement, tokens)


def pack_scaled(slots, weights, cotangent, total):
    top, tok_dev = slots.shape
    width = cotangent.shape[1]
    block = min(total, 256)
    return pl.pallas_call(
        scaled_kernel,
        grid=(total // block,),
        in_specs=[whole((top, tok_dev)), whole((top, tok_dev)), whole((tok_dev, width))],
        out_specs=strip(block, width),
        out_shape=jax.ShapeDtypeStruct((total, width), BF16),
        compiler_params=params(),
        cost_estimate=cost(4 * total * tok_dev * width, 2 * total * width),
        name="pack_scaled",
    )(slots, weights, cotangent)


def forward_kernel(rows_ref, gate_ref, up_ref, down_ref, out_ref, gate_pre_ref, up_proj_ref, hidden_ref):
    inputs = rows_ref[...]
    gate_pre = dot(inputs, gate_ref[...])
    up_proj = dot(inputs, up_ref[...])
    gate_pre_ref[...] = gate_pre
    up_proj_ref[...] = up_proj
    hidden = (gate_pre * jax.nn.sigmoid(gate_pre) * up_proj).astype(BF16)
    hidden_ref[...] = hidden
    out_ref[...] = dot(hidden, down_ref[...]).astype(BF16)


def forward(rows, w_gate, w_up, w_down):
    total, width = rows.shape
    ff = w_gate.shape[1]
    block = min(total, 256)
    return pl.pallas_call(
        forward_kernel,
        grid=(total // block,),
        in_specs=[strip(block, width)] + [pl.BlockSpec(memory_space=pltpu.VMEM)] * 3,
        out_specs=[strip(block, width), strip(block, ff), strip(block, ff), strip(block, ff)],
        out_shape=[
            jax.ShapeDtypeStruct((total, width), BF16),
            jax.ShapeDtypeStruct((total, ff), F32),
            jax.ShapeDtypeStruct((total, ff), F32),
            jax.ShapeDtypeStruct((total, ff), BF16),
        ],
        compiler_params=params(),
        cost_estimate=cost(6 * total * width * ff, 4 * total * width + 6 * width * ff + 10 * total * ff),
        name="expert_forward",
    )(rows, w_gate, w_up, w_down)


def backward_kernel(rows_ref, gate_pre_ref, up_proj_ref, gate_ref, up_ref, down_ref, din_ref, dgate_ref, dup_ref):
    d_hidden = dot(rows_ref[...], down_ref[...], LAST_LAST)
    gate_pre = gate_pre_ref[...]
    sig = jax.nn.sigmoid(gate_pre)
    d_gate = (d_hidden * up_proj_ref[...] * sig * (1.0 + gate_pre * (1.0 - sig))).astype(BF16)
    d_up = (d_hidden * gate_pre * sig).astype(BF16)
    dgate_ref[...] = d_gate
    dup_ref[...] = d_up
    din_ref[...] = (
        dot(d_gate, gate_ref[...], LAST_LAST) + dot(d_up, up_ref[...], LAST_LAST)
    ).astype(BF16)


def backward(rows, gate_pre, up_proj, w_gate, w_up, w_down):
    total, width = rows.shape
    ff = w_gate.shape[1]
    block = min(total, 256)
    return pl.pallas_call(
        backward_kernel,
        grid=(total // block,),
        in_specs=[strip(block, width), strip(block, ff), strip(block, ff)]
        + [pl.BlockSpec(memory_space=pltpu.VMEM)] * 3,
        out_specs=[strip(block, width), strip(block, ff), strip(block, ff)],
        out_shape=[
            jax.ShapeDtypeStruct((total, width), BF16),
            jax.ShapeDtypeStruct((total, ff), BF16),
            jax.ShapeDtypeStruct((total, ff), BF16),
        ],
        compiler_params=params(),
        cost_estimate=cost(6 * total * width * ff, 4 * total * width + 6 * width * ff + 12 * total * ff),
        name="expert_backward",
    )(rows, gate_pre, up_proj, w_gate, w_up, w_down)


def mixed_kernel(slots_ref, weight_ref, cot_ref, out_ref, mixed_ref, groute_ref, sel_ref, dots_ref):
    step = pl.program_id(0)
    total = out_ref.shape[0]
    tok_dev = cot_ref.shape[0]
    top = slots_ref.shape[0]

    @pl.when(step == 0)
    def _():
        _, _, high, low = selectors(slots_ref[...], weight_ref[...], 0, total)
        sel_ref[:, :tok_dev] = high
        sel_ref[:, tok_dev:] = low
        dots_ref[...] = jnp.zeros_like(dots_ref)

    outcome = out_ref[...]
    halves = dot(sel_ref[...], outcome, FIRST_FIRST)
    mixed_ref[...] = (halves[:tok_dev] + halves[tok_dev:]).astype(BF16)
    dots_ref[...] += dot(outcome, cot_ref[...], LAST_LAST)

    @pl.when(step == pl.num_programs(0) - 1)
    def _():
        slots = slots_ref[...]
        row = iota((total, tok_dev), 0)
        dots = dots_ref[...]
        groute_ref[...] = jnp.concatenate(
            [
                jnp.sum(jnp.where(row == slots[k : k + 1, :], dots, 0.0), 0, keepdims=True)
                for k in range(top)
            ],
            0,
        )


def unpack_mixed(slots, weights, cotangent, outcome):
    top, tok_dev = slots.shape
    total, width = outcome.shape
    block = min(width, 512)
    return pl.pallas_call(
        mixed_kernel,
        grid=(width // block,),
        in_specs=[
            whole((top, tok_dev)),
            whole((top, tok_dev)),
            columns(tok_dev, block),
            columns(total, block),
        ],
        out_specs=[columns(tok_dev, block), whole((top, tok_dev))],
        out_shape=[
            jax.ShapeDtypeStruct((tok_dev, width), BF16),
            jax.ShapeDtypeStruct((top, tok_dev), F32),
        ],
        scratch_shapes=[
            pltpu.VMEM((total, 2 * tok_dev), BF16),
            pltpu.VMEM((total, tok_dev), F32),
        ],
        compiler_params=params(),
        cost_estimate=cost(6 * total * tok_dev * width, 2 * total * width),
        name="unpack_mixed",
    )(slots, weights, cotangent, outcome)


def gtok_kernel(chunks, slots_ref, din_ref, gtok_ref, rows_ref, part_ref, in_sems, out_sems):
    total, width = din_ref.shape
    size = width // chunks
    arrivals = []
    for i in range(chunks):
        arrivals.append(
            pltpu.make_async_copy(
                din_ref.at[:, pl.ds(i * size, size)], rows_ref.at[i], in_sems.at[i]
            )
        )
        arrivals[-1].start()
    chosen = hits_of(slots_ref[...], 0, total).T
    leaving = []
    for i in range(chunks):
        arrivals[i].wait()
        part_ref[i] = dot(chosen, rows_ref[i]).astype(BF16)
        leaving.append(
            pltpu.make_async_copy(
                part_ref.at[i], gtok_ref.at[:, pl.ds(i * size, size)], out_sems.at[i]
            )
        )
        leaving[-1].start()
    for copy in leaving:
        copy.wait()


def unpack_tokens(slots, d_inputs, chunks=UNPACK_CHUNKS):
    tok_dev = slots.shape[1]
    total, width = d_inputs.shape
    anywhere = pl.BlockSpec(memory_space=pl.ANY)
    return pl.pallas_call(
        functools.partial(gtok_kernel, chunks),
        in_specs=[pl.BlockSpec(memory_space=pltpu.VMEM), anywhere],
        out_specs=anywhere,
        out_shape=jax.ShapeDtypeStruct((tok_dev, width), BF16),
        scratch_shapes=[
            pltpu.VMEM((chunks, total, width // chunks), BF16),
            pltpu.VMEM((chunks, tok_dev, width // chunks), BF16),
            pltpu.SemaphoreType.DMA((chunks,)),
            pltpu.SemaphoreType.DMA((chunks,)),
        ],
        compiler_params=params(),
        cost_estimate=cost(2 * total * tok_dev * width, 2 * total * width),
        name="unpack_tokens",
    )(slots, d_inputs)


def exchange(buffer, experts, order):
    total, width = buffer.shape
    moved = lax.all_to_all(
        buffer.reshape(experts, total // experts, width),
        ("col", "row"),
        split_axis=0,
        concat_axis=0,
        tiled=True,
        axis_index_groups=[devices_of(order)],
    )
    return moved.reshape(total, width)


def per_device(order, tokens, route_weight, expert_ids, placement, w_gate, w_up, w_down, cotangent):
    tok_dev, width = tokens.shape
    fan_out = expert_ids.shape[1]
    experts = placement.shape[0]
    cap = max(2, min(tok_dev // 2, 8 * max(1, tok_dev * fan_out // (8 * experts))))
    weights = route_weight.T
    gate, up, down = w_gate[0], w_up[0], w_down[0]
    packed, slots = pack_tokens(
        expert_ids.T, placement.reshape(1, experts), tokens, cap, order
    )
    inputs = exchange(packed, experts, order)
    scaled = exchange(pack_scaled(slots, weights, cotangent, experts * cap), experts, order)
    outcome, gate_pre, up_proj, hidden = forward(inputs, gate, up, down)
    outcome = exchange(outcome, experts, order)
    d_inputs, d_gate, d_up = backward(scaled, gate_pre, up_proj, gate, up, down)
    returned = exchange(d_inputs, experts, order)
    grad_gate = dot(inputs, d_gate, FIRST_FIRST).astype(BF16)
    grad_up = dot(inputs, d_up, FIRST_FIRST).astype(BF16)
    grad_down = dot(hidden, scaled, FIRST_FIRST).astype(BF16)
    mixed, grad_route = unpack_mixed(slots, weights, cotangent, outcome)
    grad_tokens = unpack_tokens(slots, returned)
    return (mixed, grad_tokens, grad_route.T, grad_gate[None], grad_up[None], grad_down[None])


def solution(mesh):
    split = P(("col", "row"), None)
    split3 = P(("col", "row"), None, None)
    order = send_order(mesh.shape["col"], mesh.shape["row"])
    return jax.shard_map(
        functools.partial(per_device, order),
        mesh=mesh,
        in_specs=(split, split, split, P(), split3, split3, split3, split),
        out_specs=(split, split, split, split3, split3, split3),
        check_vma=False,
    )
```

```python
import functools
import math
import jax
import jax.numpy as jnp
import numpy as np
from jax import lax
from jax.experimental import pallas as pl
from jax.experimental.pallas import tpu as pltpu
from jax.sharding import PartitionSpec as P

BF16 = jnp.bfloat16
F32 = jnp.float32
LAST_LAST = (((1,), (1,)), ((), ()))
FIRST_FIRST = (((0,), (0,)), ((), ()))
VMEM_LIMIT = 56 * 1024 * 1024
PACK_CHUNKS = 8
UNPACK_CHUNKS = 4


def iota(shape, dim):
    return lax.broadcasted_iota(jnp.int32, shape, dim)


def dot(a, b, dims=(((1,), (0,)), ((), ()))):
    return lax.dot_general(a, b, dims, preferred_element_type=F32)


def send_order(columns_, rows_):
    side = math.isqrt(columns_)
    cores = 2 if rows_ % 2 == 0 else 1
    lines = rows_ // cores
    x = (columns_ // side, side * rows_)
    z = (side, rows_)
    y = (lines, cores)
    core = (cores, 1)
    return (x, core, z, y)


def block_of(number, order):
    block = jnp.zeros_like(number)
    for size, stride in order:
        block = block * size + (number // stride) % size
    return block


def devices_of(order):
    devices = np.zeros((1,), np.int64)
    for size, stride in order:
        devices = (devices[:, None] + np.arange(size) * stride).reshape(-1)
    return [int(device) for device in devices]


def route_slots(ids, placement, cap):
    top, tokens = ids.shape
    experts = placement.shape[1]
    expert = iota((experts, tokens), 0)
    hits = [ids[k : k + 1, :] == expert for k in range(top)]
    named = functools.reduce(jnp.logical_or, hits)
    earlier = (iota((tokens, tokens), 0) < iota((tokens, tokens), 1)).astype(F32)
    count = dot(named.astype(F32).astype(BF16), earlier.astype(BF16)).astype(jnp.int32)
    diagonal = iota((experts, experts), 0) == iota((experts, experts), 1)
    serving = jnp.sum(jnp.where(diagonal, placement, 0), 1, keepdims=True)
    slot = serving * cap + count
    return jnp.concatenate(
        [jnp.sum(jnp.where(hit, slot, 0), 0, keepdims=True) for hit in hits], 0
    )


def hits_of(slots, first, rows):
    row = iota((rows, slots.shape[1]), 0) + first
    hits = [row == slots[k : k + 1, :] for k in range(slots.shape[0])]
    return jnp.where(functools.reduce(jnp.logical_or, hits), 1.0, 0.0).astype(BF16)


def selectors(slots, weights, first, rows):
    top, tokens = slots.shape
    row = iota((rows, tokens), 0) + first
    hits = [row == slots[k : k + 1, :] for k in range(top)]
    chosen = functools.reduce(jnp.logical_or, hits)
    weight = functools.reduce(
        jnp.add, [jnp.where(hits[k], weights[k : k + 1, :], 0.0) for k in range(top)]
    )
    high = weight.astype(BF16)
    low = (weight - high.astype(F32)).astype(BF16)
    return hits, chosen.astype(F32).astype(BF16), high, low


def slots_kernel(cap, chunks, order, ids_ref, placement_ref, tokens_ref, out_ref, slots_ref, rows_ref, sems):
    size = rows_ref.shape[1]
    slots = route_slots(ids_ref[...], block_of(placement_ref[...], order), cap)
    slots_ref[...] = slots
    copies = []
    for i in range(chunks):
        chosen = hits_of(slots, i * size, size)
        rows_ref[i] = dot(chosen, tokens_ref[...]).astype(BF16)
        copies.append(
            pltpu.make_async_copy(rows_ref.at[i], out_ref.at[pl.ds(i * size, size)], sems.at[i])
        )
        copies[-1].start()
    for copy in copies:
        copy.wait()


def scaled_kernel(slots_ref, weight_ref, cot_ref, out_ref):
    rows = out_ref.shape[0]
    _, _, high, low = selectors(slots_ref[...], weight_ref[...], pl.program_id(0) * rows, rows)
    cot = cot_ref[...]
    out_ref[...] = (dot(high, cot) + dot(low, cot)).astype(BF16)


def whole(shape):
    return pl.BlockSpec(shape, lambda i: (0, 0))


def strip(block, width):
    return pl.BlockSpec((block, width), lambda i: (i, 0))


def columns(rows, block):
    return pl.BlockSpec((rows, block), lambda i: (0, i))


def params(limit=VMEM_LIMIT):
    return pltpu.CompilerParams(vmem_limit_bytes=limit)


def cost(flops, moved):
    return pl.CostEstimate(flops=flops, bytes_accessed=moved, transcendentals=0)


def pack_tokens(ids, placement, tokens, cap, order, chunks=PACK_CHUNKS):
    top, tok_dev = ids.shape
    experts = placement.shape[1]
    width = tokens.shape[1]
    total = experts * cap
    in_vmem = pl.BlockSpec(memory_space=pltpu.VMEM)
    return pl.pallas_call(
        functools.partial(slots_kernel, cap, chunks, order),
        in_specs=[in_vmem] * 3,
        out_specs=[pl.BlockSpec(memory_space=pl.ANY), in_vmem],
        out_shape=[
            jax.ShapeDtypeStruct((total, width), BF16),
            jax.ShapeDtypeStruct((top, tok_dev), jnp.int32),
        ],
        scratch_shapes=[
            pltpu.VMEM((chunks, total // chunks, width), BF16),
            pltpu.SemaphoreType.DMA((chunks,)),
        ],
        compiler_params=params(),
        name="pack_tokens",
    )(ids, placement, tokens)


def pack_scaled(slots, weights, cotangent, total):
    top, tok_dev = slots.shape
    width = cotangent.shape[1]
    block = min(total, 256)
    return pl.pallas_call(
        scaled_kernel,
        grid=(total // block,),
        in_specs=[whole((top, tok_dev)), whole((top, tok_dev)), whole((tok_dev, width))],
        out_specs=strip(block, width),
        out_shape=jax.ShapeDtypeStruct((total, width), BF16),
        compiler_params=params(),
        cost_estimate=cost(4 * total * tok_dev * width, 2 * total * width),
        name="pack_scaled",
    )(slots, weights, cotangent)


def forward_kernel(rows_ref, gate_ref, up_ref, down_ref, out_ref, gate_pre_ref, up_proj_ref, hidden_ref):
    inputs = rows_ref[...]
    gate_pre = dot(inputs, gate_ref[...])
    up_proj = dot(inputs, up_ref[...])
    gate_pre_ref[...] = gate_pre
    up_proj_ref[...] = up_proj
    hidden = (gate_pre * jax.nn.sigmoid(gate_pre) * up_proj).astype(BF16)
    hidden_ref[...] = hidden
    out_ref[...] = dot(hidden, down_ref[...]).astype(BF16)


def forward(rows, w_gate, w_up, w_down):
    total, width = rows.shape
    ff = w_gate.shape[1]
    block = min(total, 256)
    return pl.pallas_call(
        forward_kernel,
        grid=(total // block,),
        in_specs=[strip(block, width)] + [pl.BlockSpec(memory_space=pltpu.VMEM)] * 3,
        out_specs=[strip(block, width), strip(block, ff), strip(block, ff), strip(block, ff)],
        out_shape=[
            jax.ShapeDtypeStruct((total, width), BF16),
            jax.ShapeDtypeStruct((total, ff), F32),
            jax.ShapeDtypeStruct((total, ff), F32),
            jax.ShapeDtypeStruct((total, ff), BF16),
        ],
        compiler_params=params(),
        cost_estimate=cost(6 * total * width * ff, 4 * total * width + 6 * width * ff + 10 * total * ff),
        name="expert_forward",
    )(rows, w_gate, w_up, w_down)


def backward_kernel(rows_ref, gate_pre_ref, up_proj_ref, gate_ref, up_ref, down_ref, din_ref, dgate_ref, dup_ref):
    d_hidden = dot(rows_ref[...], down_ref[...], LAST_LAST)
    gate_pre = gate_pre_ref[...]
    sig = jax.nn.sigmoid(gate_pre)
    d_gate = (d_hidden * up_proj_ref[...] * sig * (1.0 + gate_pre * (1.0 - sig))).astype(BF16)
    d_up = (d_hidden * gate_pre * sig).astype(BF16)
    dgate_ref[...] = d_gate
    dup_ref[...] = d_up
    din_ref[...] = (
        dot(d_gate, gate_ref[...], LAST_LAST) + dot(d_up, up_ref[...], LAST_LAST)
    ).astype(BF16)


def backward(rows, gate_pre, up_proj, w_gate, w_up, w_down):
    total, width = rows.shape
    ff = w_gate.shape[1]
    block = min(total, 256)
    return pl.pallas_call(
        backward_kernel,
        grid=(total // block,),
        in_specs=[strip(block, width), strip(block, ff), strip(block, ff)]
        + [pl.BlockSpec(memory_space=pltpu.VMEM)] * 3,
        out_specs=[strip(block, width), strip(block, ff), strip(block, ff)],
        out_shape=[
            jax.ShapeDtypeStruct((total, width), BF16),
            jax.ShapeDtypeStruct((total, ff), BF16),
            jax.ShapeDtypeStruct((total, ff), BF16),
        ],
        compiler_params=params(),
        cost_estimate=cost(6 * total * width * ff, 4 * total * width + 6 * width * ff + 12 * total * ff),
        name="expert_backward",
    )(rows, gate_pre, up_proj, w_gate, w_up, w_down)


def mixed_kernel(slots_ref, weight_ref, cot_ref, out_ref, mixed_ref, groute_ref, sel_ref, dots_ref):
    step = pl.program_id(0)
    total = out_ref.shape[0]
    tok_dev = cot_ref.shape[0]
    top = slots_ref.shape[0]

    @pl.when(step == 0)
    def _():
        _, _, high, low = selectors(slots_ref[...], weight_ref[...], 0, total)
        sel_ref[:, :tok_dev] = high
        sel_ref[:, tok_dev:] = low
        dots_ref[...] = jnp.zeros_like(dots_ref)

    outcome = out_ref[...]
    halves = dot(sel_ref[...], outcome, FIRST_FIRST)
    mixed_ref[...] = (halves[:tok_dev] + halves[tok_dev:]).astype(BF16)
    dots_ref[...] += dot(outcome, cot_ref[...], LAST_LAST)

    @pl.when(step == pl.num_programs(0) - 1)
    def _():
        slots = slots_ref[...]
        row = iota((total, tok_dev), 0)
        dots = dots_ref[...]
        groute_ref[...] = jnp.concatenate(
            [
                jnp.sum(jnp.where(row == slots[k : k + 1, :], dots, 0.0), 0, keepdims=True)
                for k in range(top)
            ],
            0,
        )


def unpack_mixed(slots, weights, cotangent, outcome):
    top, tok_dev = slots.shape
    total, width = outcome.shape
    block = min(width, 512)
    return pl.pallas_call(
        mixed_kernel,
        grid=(width // block,),
        in_specs=[
            whole((top, tok_dev)),
            whole((top, tok_dev)),
            columns(tok_dev, block),
            columns(total, block),
        ],
        out_specs=[columns(tok_dev, block), whole((top, tok_dev))],
        out_shape=[
            jax.ShapeDtypeStruct((tok_dev, width), BF16),
            jax.ShapeDtypeStruct((top, tok_dev), F32),
        ],
        scratch_shapes=[
            pltpu.VMEM((total, 2 * tok_dev), BF16),
            pltpu.VMEM((total, tok_dev), F32),
        ],
        compiler_params=params(),
        cost_estimate=cost(6 * total * tok_dev * width, 2 * total * width),
        name="unpack_mixed",
    )(slots, weights, cotangent, outcome)


def gtok_kernel(chunks, slots_ref, din_ref, gtok_ref, rows_ref, part_ref, in_sems, out_sems):
    total, width = din_ref.shape
    size = width // chunks
    arrivals = []
    for i in range(chunks):
        arrivals.append(
            pltpu.make_async_copy(
                din_ref.at[:, pl.ds(i * size, size)], rows_ref.at[i], in_sems.at[i]
            )
        )
        arrivals[-1].start()
    chosen = hits_of(slots_ref[...], 0, total).T
    leaving = []
    for i in range(chunks):
        arrivals[i].wait()
        part_ref[i] = dot(chosen, rows_ref[i]).astype(BF16)
        leaving.append(
            pltpu.make_async_copy(
                part_ref.at[i], gtok_ref.at[:, pl.ds(i * size, size)], out_sems.at[i]
            )
        )
        leaving[-1].start()
    for copy in leaving:
        copy.wait()


def unpack_tokens(slots, d_inputs, chunks=UNPACK_CHUNKS):
    tok_dev = slots.shape[1]
    total, width = d_inputs.shape
    anywhere = pl.BlockSpec(memory_space=pl.ANY)
    return pl.pallas_call(
        functools.partial(gtok_kernel, chunks),
        in_specs=[pl.BlockSpec(memory_space=pltpu.VMEM), anywhere],
        out_specs=anywhere,
        out_shape=jax.ShapeDtypeStruct((tok_dev, width), BF16),
        scratch_shapes=[
            pltpu.VMEM((chunks, total, width // chunks), BF16),
            pltpu.VMEM((chunks, tok_dev, width // chunks), BF16),
            pltpu.SemaphoreType.DMA((chunks,)),
            pltpu.SemaphoreType.DMA((chunks,)),
        ],
        compiler_params=params(),
        cost_estimate=cost(2 * total * tok_dev * width, 2 * total * width),
        name="unpack_tokens",
    )(slots, d_inputs)


def exchange(buffer, experts, order):
    total, width = buffer.shape
    moved = lax.all_to_all(
        buffer.reshape(experts, total // experts, width),
        ("col", "row"),
        split_axis=0,
        concat_axis=0,
        tiled=True,
        axis_index_groups=[devices_of(order)],
    )
    return moved.reshape(total, width)


def per_device(order, tokens, route_weight, expert_ids, placement, w_gate, w_up, w_down, cotangent):
    tok_dev, width = tokens.shape
    fan_out = expert_ids.shape[1]
    experts = placement.shape[0]
    cap = max(2, min(tok_dev // 2, 8 * max(1, tok_dev * fan_out // (8 * experts))))
    weights = route_weight.T
    gate, up, down = w_gate[0], w_up[0], w_down[0]
    packed, slots = pack_tokens(
        expert_ids.T, placement.reshape(1, experts), tokens, cap, order
    )
    inputs = exchange(packed, experts, order)
    scaled = exchange(pack_scaled(slots, weights, cotangent, experts * cap), experts, order)
    outcome, gate_pre, up_proj, hidden = forward(inputs, gate, up, down)
    outcome = exchange(outcome, experts, order)
    d_inputs, d_gate, d_up = backward(scaled, gate_pre, up_proj, gate, up, down)
    returned = exchange(d_inputs, experts, order)
    grad_gate = dot(inputs, d_gate, FIRST_FIRST).astype(BF16)
    grad_up = dot(inputs, d_up, FIRST_FIRST).astype(BF16)
    grad_down = dot(hidden, scaled, FIRST_FIRST).astype(BF16)
    mixed, grad_route = unpack_mixed(slots, weights, cotangent, outcome)
    grad_tokens = unpack_tokens(slots, returned)
    return (mixed, grad_tokens, grad_route.T, grad_gate[None], grad_up[None], grad_down[None])


def solution(mesh):
    split = P(("col", "row"), None)
    split3 = P(("col", "row"), None, None)
    order = send_order(mesh.shape["col"], mesh.shape["row"])
    return jax.shard_map(
        functools.partial(per_device, order),
        mesh=mesh,
        in_specs=(split, split, split, P(), split3, split3, split3, split),
        out_specs=(split, split, split, split3, split3, split3),
        check_vma=False,
    )
```
